32 devices in a mesh: ens: 4 (over x, core), polar: 8 (over z, y).
Axes of the slice: x: 2, y: 2, z: 4, core: 2. Of those that a mesh axis runs over, the one named last changes fastest.
Arguments:
- field: bfloat16 [4, 48, 96, 720], P('ens', 'polar'), may hold values from -6 to 6
- target: bfloat16 [48, 96, 720], P('polar'), may hold values from -6 to 6
- slot_orders: int32 [360], replicated, may hold values from 0 to 359, each once
- analysis: bfloat16 [360, 48, 360], P('polar'), may hold values from -0.875 to 0.875
- synthesis: bfloat16 [360, 360, 48], P('polar'), may hold values from -0.3125 to 0.3125
- degree_filter: float32 [96, 360], replicated, may hold values from -4 to 4
Outputs:
- prediction: bfloat16 [4, 48, 96, 720], P('ens', 'polar')
- gradient: bfloat16 [4, 48, 96, 720], P('ens', 'polar')
The draws below stay inside these ranges and needn't reach their ends.
Inputs may be any that keep to these rules, and one draw needn't show every extreme that they name: `slot_orders`: each slot number 0 to 359 appears once; a slot whose order is 360 or more is empty.
All inputs are finite; a program needn't handle non-finite values.
Results may differ from the reference program's by a relative error of at most 0.006.
Values may be sent and summed in bfloat16 or wider, within the bound.
A program may use at most 64 MiB of HBM per device.

```python
import math
import jax
import jax.numpy as jnp
from jax import lax

NLON = 720
MAX_DEGREE = 360
CW = 96
ENS = 4
C = 96
LATITUDE_COUNT = 48
ORDER_SLOTS = 360
N_ENS = 4


def block_scale(key, extent, cuts, least, high):
    def one(position, shards_of):
        draws = jax.random.uniform(jax.random.fold_in(jax.random.fold_in(key, 6), position), (shards_of,), jnp.float32, least / len(cuts), high / len(cuts))
        return jnp.repeat(jnp.exp(draws), extent[position] // shards_of).reshape((-1,) + (1,) * (len(extent) - position - 1))

    loudness = one(*cuts[0])
    for cut in cuts[1:]:
        loudness = loudness * one(*cut)
    return loudness


def centred(own_key, dims, deviation, bound, shards=(), kind=jnp.bfloat16):
    loudness = block_scale(own_key, dims, shards, -0.22, 0.18) if shards else 1.0
    array = jax.random.normal(own_key, dims, jnp.float32) * deviation * loudness
    return jnp.minimum(jnp.maximum(array, -bound), bound).astype(kind)


def setup_inputs(seed: int = 0) -> dict:
    arg_keys = jax.random.split(jax.random.key(seed), 7)
    return {
        "field": centred(arg_keys[0], (N_ENS, LATITUDE_COUNT, CW, NLON), 1.0, 6.0, ((0, 4), (1, 8))),
        "target": centred(arg_keys[1], (LATITUDE_COUNT, C, NLON), 1.0, 6.0, ((0, 8),)),
        "slot_orders": jax.random.permutation(arg_keys[2], ORDER_SLOTS).astype(jnp.int32),
        "analysis": centred(arg_keys[3], (ORDER_SLOTS, LATITUDE_COUNT, MAX_DEGREE), LATITUDE_COUNT ** -0.5, 0.875, ((0, 8),)),
        "synthesis": centred(arg_keys[4], (ORDER_SLOTS, MAX_DEGREE, LATITUDE_COUNT), MAX_DEGREE ** -0.5, 0.3125, ((0, 8),)),
        "degree_filter": centred(arg_keys[5], (C, MAX_DEGREE), 1.0, 4.0, (), jnp.float32),
    }


smooth_sq = 0.25

def lon_tables(slot_orders, lon_count, degree_total):
    orders = slot_orders.astype(jnp.int32)
    points = jnp.arange(lon_count, dtype=jnp.int32)
    phase = orders[:, None] * points[None, :] % lon_count
    angle = phase.astype(jnp.float32) * (2.0 * math.pi / lon_count)
    live = (orders < degree_total).astype(jnp.float32)[:, None]
    cosine = jnp.cos(angle) * live
    sine = jnp.sin(angle) * live
    paired = jnp.stack([cosine, -sine], 1)
    forward = (paired / math.sqrt(lon_count)).astype(jnp.bfloat16)
    inverse = (paired / math.sqrt(degree_total)).astype(jnp.bfloat16)
    return (forward, inverse)

def kernel_slope(diff):
    return diff / jnp.sqrt(diff * diff + smooth_sq)

def reference(field, target, slot_orders, analysis, synthesis, degree_filter):
    slab_count, lat_count, chan_count, lon_count = field.shape
    group_count = slab_count // ENS
    slot_count, degree_total = (analysis.shape[0], analysis.shape[2])
    forward, inverse = lon_tables(slot_orders, lon_count, degree_total)
    degrees = jnp.arange(degree_total, dtype=jnp.int32)
    keeping = (degrees[None, :] >= slot_orders.astype(jnp.int32)[:, None]).astype(jnp.float32)
    filters = degree_filter.astype(jnp.float32).reshape(group_count, chan_count, degree_total)
    slab_weights = jnp.repeat(filters, ENS, axis=0)
    flat_forward = forward.reshape(slot_count * 2, lon_count).T

    def one_member(inputs):
        member, rows = inputs
        scaling = rows[None, None] * keeping[:, None, None, :]
        flat = member.reshape(lat_count * chan_count, lon_count)
        spectral = jnp.dot(flat, flat_forward, preferred_element_type=jnp.float32).astype(jnp.bfloat16)
        spectral = spectral.reshape(lat_count, chan_count, slot_count, 2).transpose(2, 3, 1, 0)
        coeffs = jnp.einsum('spct,stl->spcl', spectral.astype(jnp.float32), analysis.astype(jnp.float32))
        scaled = (coeffs * scaling).astype(jnp.bfloat16)
        bands = jnp.einsum('spcl,slt->spct', scaled.astype(jnp.float32), synthesis.astype(jnp.float32)).astype(jnp.bfloat16)
        synth = jnp.einsum('spct,spk->tck', bands.astype(jnp.float32), inverse.astype(jnp.float32))
        return (member.astype(jnp.float32) + synth).astype(jnp.bfloat16)
    prediction = lax.map(one_member, (field, slab_weights))

    def per_cycle(inputs):
        members, observed = inputs
        values = members.astype(jnp.float32)
        own_term = kernel_slope(values - observed.astype(jnp.float32)[None])

        def add_member(summed, other):
            return (summed + kernel_slope(values - other[None]), None)
        pair_sum, unused = lax.scan(add_member, jnp.zeros_like(values), values)
        return (own_term - pair_sum / ENS).astype(jnp.bfloat16)
    grouped = prediction.reshape(group_count, ENS, lat_count, chan_count, lon_count)
    grouped = grouped.transpose(0, 2, 1, 3, 4).reshape(group_count * lat_count, ENS, chan_count, lon_count)
    observed = target.reshape(lat_count, group_count, chan_count, lon_count).transpose(1, 0, 2, 3)
    observed = observed.reshape(group_count * lat_count, chan_count, lon_count)
    slopes = lax.map(per_cycle, (grouped, observed))
    slopes = slopes.reshape(group_count, lat_count, ENS, chan_count, lon_count).transpose(0, 2, 1, 3, 4)
    gradient = slopes.reshape(slab_count, lat_count, chan_count, lon_count)
    return (prediction, gradient)
```

```python
import functools
import math

import jax
import jax.numpy as jnp
import numpy as np
from jax import lax
from jax.experimental import pallas as pl
from jax.experimental.pallas import tpu as pltpu
from jax.sharding import PartitionSpec as P

ENS = 4
SMOOTH_SQ = 0.25
MESH = pl.DeviceIdType.MESH
F32 = jnp.float32
BF16 = jnp.bfloat16
LANES = 128


def order_tables(lon_count, degree_total):
    phase = np.arange(degree_total)[:, None] * np.arange(lon_count)[None, :] % lon_count
    angle = phase.astype(np.float32) * np.float32(2.0 * math.pi / lon_count)
    paired = np.stack([np.cos(angle), -np.sin(angle)])
    forward = jnp.asarray((paired / np.float32(math.sqrt(lon_count))).astype(BF16))
    inverse = jnp.asarray((paired / np.float32(math.sqrt(degree_total))).astype(BF16))
    return forward, inverse


def nt_dot(a, b):
    return lax.dot_general(a, b, (((1,), (1,)), ((), ())), preferred_element_type=F32)


def kernel_slope(diff):
    return diff * lax.rsqrt(diff * diff + SMOOTH_SQ)


def kernel(
    sizes,
    field_ref, orders_ref, padded_ref, filter_ref, forward_ref,
    inverse_hbm, target_hbm, analysis_hbm, synthesis_hbm,
    pred_ref, grad_ref,
    inverse_tab, target_ref, analysis_ref, synthesis_ref,
    analysis_t, synthesis_t, filter_t, inverse_rows,
    send1, recv1, x0, x1, b0, b1, send2, recv2, members, slopes, grad_in,
    local_sem, send1_sem, recv1_sem, send2_sem, recv2_sem, send3_sem, recv3_sem, send4_sem, recv4_sem,
):
    n, lat, chan, lon, slots, padded, degrees, per_send, pair = sizes
    lat_total = n * lat
    me = lax.axis_index("polar")
    slab = lax.axis_index("ens")
    member = lax.rem(slab, ENS)
    group_base = slab - member
    chunks = lat // pair
    rows = pair * chan
    quarter = rows // ENS

    local = [
        pltpu.make_async_copy(src, dst, local_sem.at[i])
        for i, (src, dst) in enumerate(
            [
                (analysis_hbm, analysis_ref),
                (synthesis_hbm, synthesis_ref),
                (inverse_hbm, inverse_tab),
                (target_hbm, target_ref),
            ]
        )
    ]
    for copy in local:
        copy.start()

    barrier = pltpu.get_barrier_semaphore()

    @pl.loop(1, n)
    def _(step):
        pl.semaphore_signal(
            barrier, inc=1, device_id={"polar": lax.rem(me + step, n)}, device_id_type=MESH
        )

    for step in range(1, ENS):
        other = group_base + lax.rem(member + step, ENS)
        pl.semaphore_signal(barrier, inc=1, device_id={"ens": other}, device_id_type=MESH)
    pl.semaphore_wait(barrier, n - 1 + ENS - 1)

    def first_copy(slot, dest):
        return pltpu.make_async_remote_copy(
            src_ref=send1.at[dest],
            dst_ref=recv1.at[slot],
            send_sem=send1_sem.at[dest],
            recv_sem=recv1_sem.at[slot],
            device_id={"polar": dest},
            device_id_type=MESH,
        )

    def second_copy(slot, dest, chunk):
        return pltpu.make_async_remote_copy(
            src_ref=send2.at[chunk, dest],
            dst_ref=recv2.at[chunk, slot],
            send_sem=send2_sem.at[chunk, dest],
            recv_sem=recv2_sem.at[chunk, slot],
            device_id={"polar": dest},
            device_id_type=MESH,
        )

    def row_start(chunk, owner):
        return pl.multiple_of(chunk * rows + owner * quarter, 16)

    def member_copy(slot, dest, chunk):
        return pltpu.make_async_remote_copy(
            src_ref=pred_buf_at(chunk, dest),
            dst_ref=members.at[chunk, slot],
            send_sem=send3_sem.at[chunk, dest],
            recv_sem=recv3_sem.at[chunk, slot],
            device_id={"ens": group_base + dest},
            device_id_type=MESH,
        )

    def pred_buf_at(chunk, dest):
        return pred_ref.at[pl.ds(row_start(chunk, dest), quarter)]

    def slope_copy(slot, dest, chunk):
        return pltpu.make_async_remote_copy(
            src_ref=slopes.at[chunk, dest],
            dst_ref=grad_in.at[pl.ds(row_start(chunk, slot), quarter)],
            send_sem=send4_sem.at[chunk, dest],
            recv_sem=recv4_sem.at[chunk, slot],
            device_id={"ens": group_base + dest},
            device_id_type=MESH,
        )

    def one_hot(block):
        ids = lax.broadcasted_iota(jnp.int32, (block.shape[0], degrees), 1)
        return jnp.where(ids == block, 1.0, 0.0).astype(BF16)

    def selected(hot, table):
        return jnp.dot(hot, table, preferred_element_type=F32).astype(BF16)

    batches = n // per_send
    mine = me // per_send

    @pl.loop(0, batches)
    def _(i):
        batch = lax.rem(mine + i, batches)
        first = batch * per_send
        span = per_send * padded
        hot = one_hot(padded_ref[pl.ds(pl.multiple_of(first * padded, 16), span), :])
        real = nt_dot(selected(hot, forward_ref[0]), field_ref[...])
        imag = nt_dot(selected(hot, forward_ref[1]), field_ref[...])
        both = jnp.concatenate([real, imag], axis=1).astype(BF16)
        for j in range(per_send):
            send1[first + j] = both[j * padded : (j + 1) * padded]

        @pl.loop(0, per_send)
        def _(j):
            dest = first + lax.rem(me + j, per_send)

            @pl.when(dest != me)
            def _():
                first_copy(me, dest).start()

    local[0].wait()
    local[1].wait()
    local[2].wait()
    local[3].wait()

    @pl.loop(0, slots)
    def _(s):
        order = orders_ref[me * slots + s]
        table = jnp.transpose(analysis_ref[s].astype(F32))
        degree = lax.broadcasted_iota(jnp.int32, table.shape, 0)
        analysis_t[s] = jnp.where(degree >= order, table, 0.0).astype(BF16)
        synthesis_t[s] = jnp.transpose(synthesis_ref[s].astype(F32)).astype(BF16)

    turned = jnp.transpose(filter_ref[...])
    filter_t[...] = jnp.zeros_like(filter_t)
    filter_t[:, 0:chan] = turned
    filter_t[:, LANES : LANES + chan] = turned

    @pl.loop(0, batches)
    def _(i):
        span = per_send * padded
        at = pl.ds(pl.multiple_of(i * span, 16), span)
        hot = one_hot(padded_ref[at, :])
        inverse_rows[0, at] = selected(hot, inverse_tab[0])
        inverse_rows[1, at] = selected(hot, inverse_tab[1])

    b0[...] = jnp.zeros_like(b0)
    b1[...] = jnp.zeros_like(b1)

    recv1[me] = send1[me]

    @pl.loop(0, n)
    def _(src):
        @pl.when(src != me)
        def _():
            first_copy(src, src).wait_recv()

        block = recv1[src].astype(F32)
        for t in range(lat):
            at = pl.ds(pl.multiple_of((src * lat + t) * padded, 16), padded)
            x0[at, 0:chan] = block[:, t * chan : (t + 1) * chan]
            x1[at, 0:chan] = block[:, (lat + t) * chan : (lat + t + 1) * chan]

    def legendre(s, carry):
        at = pl.ds(s, lat_total, stride=padded)
        values = jnp.concatenate([x0[at, :], x1[at, :]], axis=1).astype(BF16)
        coeffs = jnp.dot(analysis_t[s], values, preferred_element_type=F32)
        scaled = (coeffs * filter_t[...]).astype(BF16)
        bands = jnp.dot(synthesis_t[s], scaled, preferred_element_type=F32)
        b0[at, :] = bands[:, :LANES]
        b1[at, :] = bands[:, LANES:]
        return carry

    lax.fori_loop(0, slots, legendre, 0, unroll=3 if slots % 3 == 0 else 1)

    for chunk in range(chunks):

        @pl.loop(0, n)
        def _(step):
            dest = lax.rem(me + 1 + step, n)
            parts = []
            for source in (b0, b1):
                for t in range(pair):
                    at = (dest * lat + chunk * pair + t) * padded
                    parts.append(source[pl.ds(pl.multiple_of(at, 16), padded), 0:chan])
            send2[chunk, dest] = jnp.concatenate(parts, axis=1).astype(BF16)

            @pl.when(dest != me)
            def _():
                second_copy(me, dest, chunk).start()

    def invert(chunk):
        recv2[chunk, me] = send2[chunk, me]

        @pl.loop(1, n)
        def _(step):
            src = lax.rem(me + step, n)
            second_copy(src, src, chunk).wait_recv()

        bands = recv2[chunk].reshape(n * padded, 2 * rows)
        turned = jnp.transpose(bands.astype(F32)).astype(BF16)
        synth = jnp.dot(turned[:rows], inverse_rows[0], preferred_element_type=F32)
        synth = synth + jnp.dot(turned[rows:], inverse_rows[1], preferred_element_type=F32)
        at = pl.ds(chunk * rows, rows)
        pred_ref[at, :] = (field_ref[at, :].astype(F32) + synth).astype(BF16)
        for step in range(1, ENS):
            member_copy(member, lax.rem(member + step, ENS), chunk).start()

    def score(chunk):
        own = pl.ds(row_start(chunk, member), quarter)
        members[chunk, member] = pred_ref[own, :]
        for step in range(1, ENS):
            source = lax.rem(member + step, ENS)
            member_copy(source, source, chunk).wait_recv()

        @pl.loop(0, quarter // 16)
        def _(i):
            start = pl.multiple_of(i * 16, 16)
            at = pl.ds(start, 16)
            seen = target_ref[pl.ds(row_start(chunk, member) + start, 16), :].astype(F32)
            values = [members[chunk, e, at, :].astype(F32) for e in range(ENS)]
            pairs = [jnp.zeros_like(seen) for _ in range(ENS)]
            for a in range(ENS):
                for b in range(a + 1, ENS):
                    slope = kernel_slope(values[a] - values[b])
                    pairs[a] = pairs[a] + slope
                    pairs[b] = pairs[b] - slope
            for e in range(ENS):
                total = kernel_slope(values[e] - seen) - pairs[e] / ENS
                slopes[chunk, e, at, :] = total.astype(BF16)

        for step in range(1, ENS):
            slope_copy(member, lax.rem(member + step, ENS), chunk).start()
        grad_in[own, :] = slopes[chunk, member]

    for chunk in range(chunks):
        invert(chunk)
        if chunk:
            score(chunk - 1)
    score(chunks - 1)

    for chunk in range(chunks):
        for step in range(1, ENS):
            other = lax.rem(member + step, ENS)
            slope_copy(other, other, chunk).wait_recv()
    grad_ref[...] = grad_in[...]

    @pl.loop(1, n)
    def _(step):
        dest = lax.rem(me + step, n)
        first_copy(me, dest).wait_send()
        for chunk in range(chunks):
            second_copy(me, dest, chunk).wait_send()

    for chunk in range(chunks):
        for step in range(1, ENS):
            other = lax.rem(member + step, ENS)
            member_copy(member, other, chunk).wait_send()
            slope_copy(member, other, chunk).wait_send()


def body(field, target, slot_orders, analysis, synthesis, degree_filter):
    lat, chan, lon = field.shape[1:]
    slots, lat_total, degrees = analysis.shape
    n = lax.axis_size("polar")
    group_count = lax.axis_size("ens") // ENS
    padded = -(-slots // 16) * 16
    per_send = max(d for d in range(1, n + 1) if n % d == 0 and (d == 1 or d * padded <= 192))
    pair = 2 if lat % 2 == 0 else 1
    chunks = lat // pair
    rows = pair * chan
    quarter = rows // ENS
    forward, inverse = order_tables(lon, degrees)
    padded_orders = jnp.pad(
        slot_orders.reshape(n, slots), ((0, 0), (0, padded - slots)), constant_values=-1
    ).reshape(n * padded, 1)
    observed = target
    filters = degree_filter
    if group_count > 1:
        start = lax.axis_index("ens") // ENS * chan
        observed = lax.dynamic_slice_in_dim(target, start, chan, 1)
        filters = lax.dynamic_slice_in_dim(degree_filter, start, chan, 0)
    sizes = (n, lat, chan, lon, slots, padded, degrees, per_send, pair)
    vmem = pl.BlockSpec(memory_space=pltpu.VMEM)
    smem = pl.BlockSpec(memory_space=pltpu.SMEM)
    anywhere = pl.BlockSpec(memory_space=pl.ANY)
    dma = pltpu.SemaphoreType.DMA
    flat = jax.ShapeDtypeStruct((lat * chan, lon), BF16)
    prediction, gradient = pl.pallas_call(
        functools.partial(kernel, sizes),
        out_shape=(flat, flat),
        in_specs=[vmem, smem, vmem, vmem, vmem, anywhere, anywhere, anywhere, anywhere],
        out_specs=(vmem, vmem),
        scratch_shapes=[
            pltpu.VMEM(inverse.shape, BF16),
            pltpu.VMEM((lat * chan, lon), BF16),
            pltpu.VMEM(analysis.shape, BF16),
            pltpu.VMEM(synthesis.shape, BF16),
            pltpu.VMEM((slots, degrees, lat_total), BF16),
            pltpu.VMEM((slots, lat_total, degrees), BF16),
            pltpu.VMEM((degrees, 2 * LANES), F32),
            pltpu.VMEM((2, n * padded, lon), BF16),
            pltpu.VMEM((n, padded, 2 * lat * chan), BF16),
            pltpu.VMEM((n, padded, 2 * lat * chan), BF16),
            pltpu.VMEM((lat_total * padded, LANES), F32),
            pltpu.VMEM((lat_total * padded, LANES), F32),
            pltpu.VMEM((lat_total * padded, LANES), F32),
            pltpu.VMEM((lat_total * padded, LANES), F32),
            pltpu.VMEM((chunks, n, padded, 2 * rows), BF16),
            pltpu.VMEM((chunks, n, padded, 2 * rows), BF16),
            pltpu.VMEM((chunks, ENS, quarter, lon), BF16),
            pltpu.VMEM((chunks, ENS, quarter, lon), BF16),
            pltpu.VMEM((lat * chan, lon), BF16),
            dma((4,)),
            dma((n,)),
            dma((n,)),
            dma((chunks, n)),
            dma((chunks, n)),
            dma((chunks, ENS)),
            dma((chunks, ENS)),
            dma((chunks, ENS)),
            dma((chunks, ENS)),
        ],
        compiler_params=pltpu.CompilerParams(
            collective_id=0, has_side_effects=True, vmem_limit_bytes=56 * 1024 * 1024
        ),
    )(
        field.reshape(lat * chan, lon),
        slot_orders,
        padded_orders,
        filters,
        forward,
        inverse,
        observed.reshape(lat * chan, lon),
        analysis,
        synthesis,
    )
    return prediction.reshape(field.shape), gradient.reshape(field.shape)


def solution(mesh):
    in_specs = (
        P("ens", "polar", None, None),
        P("polar", None, None),
        P(),
        P("polar", None, None),
        P("polar", None, None),
        P(),
    )
    out_specs = (P("ens", "polar", None, None), P("ens", "polar", None, None))
    return jax.shard_map(body, mesh=mesh, in_specs=in_specs, out_specs=out_specs, check_vma=False)
```

```python
import functools
import math

import jax
import jax.numpy as jnp
import numpy as np
from jax import lax
from jax.experimental import pallas as pl
from jax.experimental.pallas import tpu as pltpu
from jax.sharding import PartitionSpec as P

ENS = 4
SMOOTH_SQ = 0.25
MESH = pl.DeviceIdType.MESH
F32 = jnp.float32
BF16 = jnp.bfloat16
LANES = 128
TILE = 16


def order_tables(lon_count, degree_total):
    phase = np.arange(degree_total)[:, None] * np.arange(lon_count)[None, :] % lon_count
    angle = phase.astype(np.float32) * np.float32(2.0 * math.pi / lon_count)
    paired = np.stack([np.cos(angle), -np.sin(angle)])
    forward = jnp.asarray((paired / np.float32(math.sqrt(lon_count))).astype(BF16))
    inverse = jnp.asarray((paired / np.float32(math.sqrt(degree_total))).astype(BF16))
    return forward, inverse


def nt_dot(a, b):
    return lax.dot_general(a, b, (((1,), (1,)), ((), ())), preferred_element_type=F32)


def kernel_slope(diff):
    return diff * lax.rsqrt(diff * diff + SMOOTH_SQ)


def kernel(
    sizes,
    field_hbm, orders_ref, order_row_ref, filter_ref, forward_hbm,
    inverse_hbm, target_hbm, analysis_hbm, synthesis_ref_hbm,
    pred_hbm, grad_hbm,
    field_ref, forward_ref, inverse_tab, target_ref, analysis_ref, synthesis_ref,
    analysis_t, filter_t, inverse_rows,
    send1, recv1, x0, x1, b0, b1, send2, recv2, pred_ref, members, slopes, grad_in,
    local_sem, out_sem, send1_sem, recv1_sem, send2_sem, recv2_sem,
    send3_sem, recv3_sem, send4_sem, recv4_sem,
):
    n, lat, chan, slots, groups, per_group, degrees, per_send, pair = sizes
    lat_total = n * lat
    padded = groups * TILE
    me = lax.axis_index("polar")
    slab = lax.axis_index("ens")
    member = lax.rem(slab, ENS)
    group_base = slab - member
    chunks = lat // pair
    rows = pair * chan
    quarter = rows // ENS

    pairs_in = [
        (forward_hbm, forward_ref),
        (field_hbm, field_ref),
        (analysis_hbm, analysis_ref),
        (inverse_hbm, inverse_tab),
        (synthesis_ref_hbm, synthesis_ref),
        (target_hbm, target_ref),
    ]
    local = [
        pltpu.make_async_copy(src, dst, local_sem.at[i]) for i, (src, dst) in enumerate(pairs_in)
    ]
    for copy in local:
        copy.start()

    barrier = pltpu.get_barrier_semaphore()

    @pl.loop(1, n)
    def _(step):
        pl.semaphore_signal(
            barrier, inc=1, device_id={"polar": lax.rem(me + step, n)}, device_id_type=MESH
        )

    for step in range(1, ENS):
        other = group_base + lax.rem(member + step, ENS)
        pl.semaphore_signal(barrier, inc=1, device_id={"ens": other}, device_id_type=MESH)

    def first_copy(slot, dest, group):
        return pltpu.make_async_remote_copy(
            src_ref=send1.at[group, dest],
            dst_ref=recv1.at[group, slot],
            send_sem=send1_sem.at[group, dest],
            recv_sem=recv1_sem.at[group, slot],
            device_id={"polar": dest},
            device_id_type=MESH,
        )

    def second_copy(slot, dest, chunk):
        return pltpu.make_async_remote_copy(
            src_ref=send2.at[chunk, dest],
            dst_ref=recv2.at[chunk, slot],
            send_sem=send2_sem.at[chunk, dest],
            recv_sem=recv2_sem.at[chunk, slot],
            device_id={"polar": dest},
            device_id_type=MESH,
        )

    def row_start(chunk, owner):
        return pl.multiple_of(chunk * rows + owner * quarter, TILE)

    def member_copy(slot, dest, chunk):
        return pltpu.make_async_remote_copy(
            src_ref=pred_ref.at[pl.ds(row_start(chunk, dest), quarter)],
            dst_ref=members.at[chunk, slot],
            send_sem=send3_sem.at[chunk, dest],
            recv_sem=recv3_sem.at[chunk, slot],
            device_id={"ens": group_base + dest},
            device_id_type=MESH,
        )

    def slope_copy(slot, dest, chunk):
        return pltpu.make_async_remote_copy(
            src_ref=slopes.at[chunk, dest],
            dst_ref=grad_in.at[pl.ds(row_start(chunk, slot), quarter)],
            send_sem=send4_sem.at[chunk, dest],
            recv_sem=recv4_sem.at[chunk, slot],
            device_id={"ens": group_base + dest},
            device_id_type=MESH,
        )

    def out_copy(which, chunk):
        source, dest = ((pred_ref, pred_hbm), (grad_in, grad_hbm))[which]
        at = pl.ds(chunk * rows, rows)
        return pltpu.make_async_copy(source.at[at], dest.at[at], out_sem.at[which, chunk])

    order_row = order_row_ref[...].astype(F32)

    def one_hot(device, group, rank):
        slot = group * per_group + rank
        live = (rank < per_group) & (slot < slots)
        slot = jnp.where(live, device * slots + slot, -1)
        ids = lax.broadcasted_iota(jnp.int32, (slot.shape[0], order_row.shape[1]), 1)
        picked = jnp.where(ids == slot, order_row + 1.0, 0.0)
        order = jnp.sum(picked, axis=1, keepdims=True) - 1.0
        ids = lax.broadcasted_iota(jnp.int32, (slot.shape[0], degrees), 1).astype(F32)
        return jnp.where(ids == order, 1.0, 0.0).astype(BF16)

    def selected(hot, table):
        return jnp.dot(hot, table, preferred_element_type=F32).astype(BF16)

    batches = n // per_send
    span = per_send * TILE

    def column(count):
        return lax.broadcasted_iota(jnp.int32, (count, 1), 0)

    def spectral(group, batch):
        first = batch * per_send
        position = column(span)
        hot = one_hot(first + position // TILE, group, lax.rem(position, TILE))
        table = jnp.concatenate([selected(hot, forward_ref[0]), selected(hot, forward_ref[1])], 0)
        values = nt_dot(table, field_ref[...])
        both = jnp.concatenate([values[:span], values[span:]], axis=1).astype(BF16)
        for j in range(per_send):
            send1[group, first + j] = both[j * TILE : (j + 1) * TILE]

    def dispatch(group, batch):
        first = batch * per_send

        @pl.loop(0, per_send)
        def _(j):
            dest = first + lax.rem(me + 1 + j, per_send)

            @pl.when(dest != me)
            def _():
                first_copy(me, dest, group).start()

    local[0].wait()
    local[1].wait()
    spectral(0, 0)
    pl.semaphore_wait(barrier, n - 1 + ENS - 1)
    dispatch(0, 0)

    @pl.loop(1, groups * batches)
    def _(i):
        spectral(i // batches, lax.rem(i, batches))
        dispatch(i // batches, lax.rem(i, batches))

    local[2].wait()

    @pl.loop(0, slots)
    def _(s):
        order = orders_ref[me * slots + s]
        table = jnp.transpose(analysis_ref[s].astype(F32))
        degree = lax.broadcasted_iota(jnp.int32, table.shape, 0)
        analysis_t[s] = jnp.where(degree >= order, table, 0.0).astype(BF16)

    turned = jnp.transpose(filter_ref[...])
    filter_t[...] = jnp.zeros_like(filter_t)
    filter_t[:, 0:chan] = turned
    filter_t[:, LANES : LANES + chan] = turned
    b0[...] = jnp.zeros_like(b0)
    b1[...] = jnp.zeros_like(b1)
    local[3].wait()
    local[4].wait()
    local[5].wait()

    def turn_inverse():
        @pl.loop(0, n)
        def _(device):
            position = column(padded)
            hot = one_hot(device, position // TILE, lax.rem(position, TILE))
            at = pl.ds(pl.multiple_of(device * padded, TILE), padded)
            inverse_rows[0, at] = selected(hot, inverse_tab[0])
            inverse_rows[1, at] = selected(hot, inverse_tab[1])

    turn_inverse()

    for group in range(groups):
        recv1[group, me] = send1[group, me]

        @pl.loop(0, n)
        def _(src):
            @pl.when(src != me)
            def _():
                first_copy(src, src, group).wait_recv()

            block = recv1[group, src].astype(F32)
            for t in range(lat):
                at = pl.ds(pl.multiple_of((src * lat + t) * TILE, TILE), TILE)
                x0[at, 0:chan] = block[:, t * chan : (t + 1) * chan]
                x1[at, 0:chan] = block[:, (lat + t) * chan : (lat + t + 1) * chan]

        base = group * lat_total * TILE

        def legendre(rank, carry):
            s = group * per_group + rank
            at = pl.ds(rank, lat_total, stride=TILE)
            values = jnp.concatenate([x0[at, :], x1[at, :]], axis=1).astype(BF16)
            coeffs = jnp.dot(analysis_t[s], values, preferred_element_type=F32)
            scaled = (coeffs * filter_t[...]).astype(BF16)
            bands = jnp.dot(synthesis_ref[s], scaled, preferred_element_type=F32)
            out = pl.ds(base + rank, lat_total, stride=TILE)
            b0[out, :] = bands[:, :LANES]
            b1[out, :] = bands[:, LANES:]
            return carry

        count = min(per_group, slots - group * per_group)
        unroll = max(u for u in (1, 2, 3, 4, 5) if count % u == 0)
        lax.fori_loop(0, count, legendre, 0, unroll=unroll)

        for chunk in range(chunks):

            @pl.loop(0, n)
            def _(step):
                dest = lax.rem(me + 1 + step, n)
                parts = []
                for source in (b0, b1):
                    for t in range(pair):
                        at = base + (dest * lat + chunk * pair + t) * TILE
                        parts.append(source[pl.ds(pl.multiple_of(at, TILE), TILE), 0:chan])
                send2[chunk, dest, group * TILE : (group + 1) * TILE, :] = jnp.concatenate(
                    parts, axis=1
                ).astype(BF16)

                if group == groups - 1:

                    @pl.when(dest != me)
                    def _():
                        second_copy(me, dest, chunk).start()

    def invert(chunk):
        recv2[chunk, me] = send2[chunk, me]

        @pl.loop(1, n)
        def _(step):
            src = lax.rem(me + step, n)
            second_copy(src, src, chunk).wait_recv()

        bands = recv2[chunk].reshape(n * padded, 2 * rows)
        turned = jnp.transpose(bands.astype(F32)).astype(BF16)
        synth = jnp.dot(turned[:rows], inverse_rows[0], preferred_element_type=F32)
        synth = synth + jnp.dot(turned[rows:], inverse_rows[1], preferred_element_type=F32)
        at = pl.ds(chunk * rows, rows)
        pred_ref[at, :] = (field_ref[at, :].astype(F32) + synth).astype(BF16)
        for step in range(1, ENS):
            member_copy(member, lax.rem(member + step, ENS), chunk).start()
        out_copy(0, chunk).start()

    def score(chunk):
        own = pl.ds(row_start(chunk, member), quarter)
        members[chunk, member] = pred_ref[own, :]
        for step in range(1, ENS):
            source = lax.rem(member + step, ENS)
            member_copy(source, source, chunk).wait_recv()

        @pl.loop(0, quarter // TILE)
        def _(i):
            start = pl.multiple_of(i * TILE, TILE)
            at = pl.ds(start, TILE)
            seen = target_ref[pl.ds(row_start(chunk, member) + start, TILE), :].astype(F32)
            values = [members[chunk, e, at, :].astype(F32) for e in range(ENS)]
            pairs = [jnp.zeros_like(seen) for _ in range(ENS)]
            for a in range(ENS):
                for b in range(a + 1, ENS):
                    slope = kernel_slope(values[a] - values[b])
                    pairs[a] = pairs[a] + slope
                    pairs[b] = pairs[b] - slope
            for e in range(ENS):
                total = kernel_slope(values[e] - seen) - pairs[e] / ENS
                slopes[chunk, e, at, :] = total.astype(BF16)

        for step in range(1, ENS):
            slope_copy(member, lax.rem(member + step, ENS), chunk).start()
        grad_in[own, :] = slopes[chunk, member]

    def collect(chunk):
        for step in range(1, ENS):
            other = lax.rem(member + step, ENS)
            slope_copy(other, other, chunk).wait_recv()
        out_copy(1, chunk).start()

    for chunk in range(chunks):
        invert(chunk)
        if chunk:
            score(chunk - 1)
    score(chunks - 1)

    @pl.loop(1, n)
    def _(step):
        dest = lax.rem(me + step, n)
        for group in range(groups):
            first_copy(me, dest, group).wait_send()
        for chunk in range(chunks):
            second_copy(me, dest, chunk).wait_send()

    for chunk in range(chunks):
        collect(chunk)
    for chunk in range(chunks):
        for step in range(1, ENS):
            other = lax.rem(member + step, ENS)
            member_copy(member, other, chunk).wait_send()
            slope_copy(member, other, chunk).wait_send()
        out_copy(0, chunk).wait()
        out_copy(1, chunk).wait()


def body(field, target, slot_orders, analysis, synthesis, degree_filter):
    lat, chan, lon = field.shape[1:]
    slots, lat_total, degrees = analysis.shape
    n = lax.axis_size("polar")
    group_count = lax.axis_size("ens") // ENS
    groups = -(-slots // TILE)
    per_group = -(-slots // groups)
    padded = groups * TILE
    per_send = max(d for d in range(1, n + 1) if n % d == 0 and (d == 1 or d * TILE <= 128))
    pair = 2 if lat % 2 == 0 else 1
    chunks = lat // pair
    rows = pair * chan
    quarter = rows // ENS
    forward, inverse = order_tables(lon, degrees)
    observed = target
    filters = degree_filter
    if group_count > 1:
        start = lax.axis_index("ens") // ENS * chan
        observed = lax.dynamic_slice_in_dim(target, start, chan, 1)
        filters = lax.dynamic_slice_in_dim(degree_filter, start, chan, 0)
    sizes = (n, lat, chan, slots, groups, per_group, degrees, per_send, pair)
    vmem = pl.BlockSpec(memory_space=pltpu.VMEM)
    smem = pl.BlockSpec(memory_space=pltpu.SMEM)
    anywhere = pl.BlockSpec(memory_space=pl.ANY)
    dma = pltpu.SemaphoreType.DMA
    flat = jax.ShapeDtypeStruct((lat * chan, lon), BF16)
    prediction, gradient = pl.pallas_call(
        functools.partial(kernel, sizes),
        out_shape=(flat, flat),
        in_specs=[anywhere, smem, vmem, vmem] + [anywhere] * 5,
        out_specs=(anywhere, anywhere),
        scratch_shapes=[
            pltpu.VMEM((lat * chan, lon), BF16),
            pltpu.VMEM(forward.shape, BF16),
            pltpu.VMEM(inverse.shape, BF16),
            pltpu.VMEM((lat * chan, lon), BF16),
            pltpu.VMEM(analysis.shape, BF16),
            pltpu.VMEM((slots, lat_total, degrees), BF16),
            pltpu.VMEM((slots, degrees, lat_total), BF16),
            pltpu.VMEM((degrees, 2 * LANES), F32),
            pltpu.VMEM((2, n * padded, lon), BF16),
            pltpu.VMEM((groups, n, TILE, 2 * lat * chan), BF16),
            pltpu.VMEM((groups, n, TILE, 2 * lat * chan), BF16),
            pltpu.VMEM((lat_total * TILE, LANES), F32),
            pltpu.VMEM((lat_total * TILE, LANES), F32),
            pltpu.VMEM((groups * lat_total * TILE, LANES), F32),
            pltpu.VMEM((groups * lat_total * TILE, LANES), F32),
            pltpu.VMEM((chunks, n, padded, 2 * rows), BF16),
            pltpu.VMEM((chunks, n, padded, 2 * rows), BF16),
            pltpu.VMEM((lat * chan, lon), BF16),
            pltpu.VMEM((chunks, ENS, quarter, lon), BF16),
            pltpu.VMEM((chunks, ENS, quarter, lon), BF16),
            pltpu.VMEM((lat * chan, lon), BF16),
            dma((6,)),
            dma((2, chunks)),
            dma((groups, n)),
            dma((groups, n)),
            dma((chunks, n)),
            dma((chunks, n)),
            dma((chunks, ENS)),
            dma((chunks, ENS)),
            dma((chunks, ENS)),
            dma((chunks, ENS)),
        ],
        compiler_params=pltpu.CompilerParams(
            collective_id=0, has_side_effects=True, vmem_limit_bytes=56 * 1024 * 1024
        ),
    )(
        field.reshape(lat * chan, lon),
        slot_orders,
        slot_orders.reshape(1, -1),
        filters,
        forward,
        inverse,
        observed.reshape(lat * chan, lon),
        analysis,
        jnp.swapaxes(synthesis, 1, 2),
    )
    return prediction.reshape(field.shape), gradient.reshape(field.shape)


def solution(mesh):
    in_specs = (
        P("ens", "polar", None, None),
        P("polar", None, None),
        P(),
        P("polar", None, None),
        P("polar", None, None),
        P(),
    )
    out_specs = (P("ens", "polar", None, None), P("ens", "polar", None, None))
    return jax.shard_map(body, mesh=mesh, in_specs=in_specs, out_specs=out_specs, check_vma=False)
```

```python
import functools
import math

import jax
import jax.numpy as jnp
import numpy as np
from jax import lax
from jax.experimental import pallas as pl
from jax.experimental.pallas import tpu as pltpu
from jax.sharding import PartitionSpec as P

ENS = 4
SMOOTH_SQ = 0.25
MESH = pl.DeviceIdType.MESH
F32 = jnp.float32
BF16 = jnp.bfloat16
LANES = 128
TILE = 16


def order_tables(lon_count, degree_total):
    phase = np.arange(degree_total)[:, None] * np.arange(lon_count)[None, :] % lon_count
    angle = phase.astype(np.float32) * np.float32(2.0 * math.pi / lon_count)
    paired = np.stack([np.cos(angle), -np.sin(angle)])
    forward = jnp.asarray((paired / np.float32(math.sqrt(lon_count))).astype(BF16))
    inverse = jnp.asarray((paired / np.float32(math.sqrt(degree_total))).astype(BF16))
    return forward, inverse


def nt_dot(a, b):
    return lax.dot_general(a, b, (((1,), (1,)), ((), ())), preferred_element_type=F32)


def kernel_slope(diff):
    return diff * lax.rsqrt(diff * diff + SMOOTH_SQ)


def kernel(
    sizes,
    field_hbm, orders_ref, order_row_ref, filter_ref, forward_hbm,
    inverse_hbm, target_hbm, analysis_hbm, synthesis_ref_hbm,
    pred_hbm, grad_hbm,
    field_ref, forward_ref, inverse_tab, target_ref, analysis_ref, synthesis_ref,
    analysis_t, filter_t, inverse_rows,
    send1, recv1, x0, x1, b0, b1, send2, recv2, pred_ref, members, slopes, grad_in,
    local_sem, out_sem, send1_sem, recv1_sem, send2_sem, recv2_sem,
    send3_sem, recv3_sem, send4_sem, recv4_sem,
):
    n, lat, chan, slots, groups, per_group, degrees, per_send, pair = sizes
    lat_total = n * lat
    padded = groups * TILE
    me = lax.axis_index("polar")
    slab = lax.axis_index("ens")
    member = lax.rem(slab, ENS)
    group_base = slab - member
    chunks = lat // pair
    rows = pair * chan
    quarter = rows // ENS

    pairs_in = [
        (forward_hbm, forward_ref),
        (field_hbm, field_ref),
        (analysis_hbm, analysis_ref),
        (inverse_hbm, inverse_tab),
        (synthesis_ref_hbm, synthesis_ref),
        (target_hbm, target_ref),
    ]
    local = [
        pltpu.make_async_copy(src, dst, local_sem.at[i]) for i, (src, dst) in enumerate(pairs_in)
    ]
    for copy in local:
        copy.start()

    barrier = pltpu.get_barrier_semaphore()

    @pl.loop(1, n)
    def _(step):
        pl.semaphore_signal(
            barrier, inc=1, device_id={"polar": lax.rem(me + step, n)}, device_id_type=MESH
        )

    for step in range(1, ENS):
        other = group_base + lax.rem(member + step, ENS)
        pl.semaphore_signal(barrier, inc=1, device_id={"ens": other}, device_id_type=MESH)

    def first_copy(slot, dest, group):
        return pltpu.make_async_remote_copy(
            src_ref=send1.at[group, dest],
            dst_ref=recv1.at[group, slot],
            send_sem=send1_sem.at[group, dest],
            recv_sem=recv1_sem.at[group, slot],
            device_id={"polar": dest},
            device_id_type=MESH,
        )

    def second_copy(slot, dest, chunk):
        return pltpu.make_async_remote_copy(
            src_ref=send2.at[chunk, dest],
            dst_ref=recv2.at[chunk, slot],
            send_sem=send2_sem.at[chunk, dest],
            recv_sem=recv2_sem.at[chunk, slot],
            device_id={"polar": dest},
            device_id_type=MESH,
        )

    def row_start(chunk, owner):
        return pl.multiple_of(chunk * rows + owner * quarter, TILE)

    def member_copy(slot, dest, chunk):
        return pltpu.make_async_remote_copy(
            src_ref=pred_ref.at[pl.ds(row_start(chunk, dest), quarter)],
            dst_ref=members.at[chunk, slot],
            send_sem=send3_sem.at[chunk, dest],
            recv_sem=recv3_sem.at[chunk, slot],
            device_id={"ens": group_base + dest},
            device_id_type=MESH,
        )

    def slope_copy(slot, dest, chunk):
        return pltpu.make_async_remote_copy(
            src_ref=slopes.at[chunk, dest],
            dst_ref=grad_in.at[pl.ds(row_start(chunk, slot), quarter)],
            send_sem=send4_sem.at[chunk, dest],
            recv_sem=recv4_sem.at[chunk, slot],
            device_id={"ens": group_base + dest},
            device_id_type=MESH,
        )

    def out_copy(which, chunk):
        source, dest = ((pred_ref, pred_hbm), (grad_in, grad_hbm))[which]
        at = pl.ds(chunk * rows, rows)
        return pltpu.make_async_copy(source.at[at], dest.at[at], out_sem.at[which, chunk])

    order_row = order_row_ref[...].astype(F32)

    def one_hot(device, group, rank):
        slot = group * per_group + rank
        live = (rank < per_group) & (slot < slots)
        slot = jnp.where(live, device * slots + slot, -1)
        ids = lax.broadcasted_iota(jnp.int32, (slot.shape[0], order_row.shape[1]), 1)
        picked = jnp.where(ids == slot, order_row + 1.0, 0.0)
        order = jnp.sum(picked, axis=1, keepdims=True) - 1.0
        ids = lax.broadcasted_iota(jnp.int32, (slot.shape[0], degrees), 1).astype(F32)
        return jnp.where(ids == order, 1.0, 0.0).astype(BF16)

    def selected(hot, table):
        return jnp.dot(hot, table, preferred_element_type=F32).astype(BF16)

    batches = n // per_send
    span = per_send * TILE

    def column(count):
        return lax.broadcasted_iota(jnp.int32, (count, 1), 0)

    def spectral(group, batch):
        first = batch * per_send
        position = column(span)
        hot = one_hot(first + position // TILE, group, lax.rem(position, TILE))
        table = jnp.concatenate([selected(hot, forward_ref[0]), selected(hot, forward_ref[1])], 0)
        values = nt_dot(table, field_ref[...])
        both = jnp.concatenate([values[:span], values[span:]], axis=1).astype(BF16)
        for j in range(per_send):
            send1[group, first + j] = both[j * TILE : (j + 1) * TILE]

    def dispatch(group, batch):
        first = batch * per_send

        @pl.loop(0, per_send)
        def _(j):
            dest = first + lax.rem(me + 1 + j, per_send)

            @pl.when(dest != me)
            def _():
                first_copy(me, dest, group).start()

    local[0].wait()
    local[1].wait()
    spectral(0, 0)
    pl.semaphore_wait(barrier, n - 1 + ENS - 1)
    dispatch(0, 0)

    @pl.loop(1, groups * batches)
    def _(i):
        spectral(i // batches, lax.rem(i, batches))
        dispatch(i // batches, lax.rem(i, batches))

    def turn_analysis(group):
        @pl.loop(group * per_group, min(slots, (group + 1) * per_group))
        def _(s):
            order = orders_ref[me * slots + s]
            table = jnp.transpose(analysis_ref[s].astype(F32))
            degree = lax.broadcasted_iota(jnp.int32, table.shape, 0)
            analysis_t[s] = jnp.where(degree >= order, table, 0.0).astype(BF16)

    turned = jnp.transpose(filter_ref[...])
    filter_t[...] = jnp.zeros_like(filter_t)
    filter_t[:, 0:chan] = turned
    filter_t[:, LANES : LANES + chan] = turned
    b0[...] = jnp.zeros_like(b0)
    b1[...] = jnp.zeros_like(b1)
    local[2].wait()
    local[4].wait()

    def turn_inverse():
        span = per_send * padded

        @pl.loop(0, batches)
        def _(batch):
            position = column(span)
            place = lax.rem(position, padded)
            hot = one_hot(batch * per_send + position // padded, place // TILE, lax.rem(place, TILE))
            at = pl.ds(pl.multiple_of(batch * span, TILE), span)
            inverse_rows[0, at] = selected(hot, inverse_tab[0])
            inverse_rows[1, at] = selected(hot, inverse_tab[1])

    for group in range(groups):
        turn_analysis(group)
        recv1[group, me] = send1[group, me]

        @pl.loop(0, n)
        def _(src):
            @pl.when(src != me)
            def _():
                first_copy(src, src, group).wait_recv()

            block = recv1[group, src].astype(F32)
            for t in range(lat):
                at = pl.ds(pl.multiple_of((src * lat + t) * TILE, TILE), TILE)
                x0[at, 0:chan] = block[:, t * chan : (t + 1) * chan]
                x1[at, 0:chan] = block[:, (lat + t) * chan : (lat + t + 1) * chan]

        base = group * lat_total * TILE

        def legendre(rank, carry):
            s = group * per_group + rank
            at = pl.ds(rank, lat_total, stride=TILE)
            values = jnp.concatenate([x0[at, :], x1[at, :]], axis=1).astype(BF16)
            coeffs = jnp.dot(analysis_t[s], values, preferred_element_type=F32)
            scaled = (coeffs * filter_t[...]).astype(BF16)
            bands = jnp.dot(synthesis_ref[s], scaled, preferred_element_type=F32)
            out = pl.ds(base + rank, lat_total, stride=TILE)
            b0[out, :] = bands[:, :LANES]
            b1[out, :] = bands[:, LANES:]
            return carry

        count = min(per_group, slots - group * per_group)
        unroll = max(u for u in (1, 2, 3, 4, 5) if count % u == 0)
        lax.fori_loop(0, count, legendre, 0, unroll=unroll)

        for chunk in range(chunks):

            @pl.loop(0, n)
            def _(step):
                dest = lax.rem(me + 1 + step, n)
                parts = []
                for source in (b0, b1):
                    for t in range(pair):
                        at = base + (dest * lat + chunk * pair + t) * TILE
                        parts.append(source[pl.ds(pl.multiple_of(at, TILE), TILE), 0:chan])
                send2[chunk, dest, group * TILE : (group + 1) * TILE, :] = jnp.concatenate(
                    parts, axis=1
                ).astype(BF16)

                if group == groups - 1:

                    @pl.when(dest != me)
                    def _():
                        second_copy(me, dest, chunk).start()

    local[3].wait()
    local[5].wait()
    turn_inverse()

    def invert(chunk):
        recv2[chunk, me] = send2[chunk, me]

        @pl.loop(1, n)
        def _(step):
            src = lax.rem(me + step, n)
            second_copy(src, src, chunk).wait_recv()

        bands = recv2[chunk].reshape(n * padded, 2 * rows)
        turned = jnp.transpose(bands.astype(F32)).astype(BF16)
        synth = jnp.dot(turned[:rows], inverse_rows[0], preferred_element_type=F32)
        synth = synth + jnp.dot(turned[rows:], inverse_rows[1], preferred_element_type=F32)
        at = pl.ds(chunk * rows, rows)
        pred_ref[at, :] = (field_ref[at, :].astype(F32) + synth).astype(BF16)
        for step in range(1, ENS):
            member_copy(member, lax.rem(member + step, ENS), chunk).start()
        out_copy(0, chunk).start()

    def score(chunk):
        own = pl.ds(row_start(chunk, member), quarter)
        members[chunk, member] = pred_ref[own, :]
        for step in range(1, ENS):
            source = lax.rem(member + step, ENS)
            member_copy(source, source, chunk).wait_recv()

        @pl.loop(0, quarter // TILE)
        def _(i):
            start = pl.multiple_of(i * TILE, TILE)
            at = pl.ds(start, TILE)
            seen = target_ref[pl.ds(row_start(chunk, member) + start, TILE), :].astype(F32)
            values = [members[chunk, e, at, :].astype(F32) for e in range(ENS)]
            pairs = [jnp.zeros_like(seen) for _ in range(ENS)]
            for a in range(ENS):
                for b in range(a + 1, ENS):
                    slope = kernel_slope(values[a] - values[b])
                    pairs[a] = pairs[a] + slope
                    pairs[b] = pairs[b] - slope
            for e in range(ENS):
                total = kernel_slope(values[e] - seen) - pairs[e] / ENS
                slopes[chunk, e, at, :] = total.astype(BF16)

        for step in range(1, ENS):
            slope_copy(member, lax.rem(member + step, ENS), chunk).start()
        grad_in[own, :] = slopes[chunk, member]

    def collect(chunk):
        for step in range(1, ENS):
            other = lax.rem(member + step, ENS)
            slope_copy(other, other, chunk).wait_recv()
        out_copy(1, chunk).start()

    for chunk in range(chunks):
        invert(chunk)
        if chunk:
            score(chunk - 1)
    score(chunks - 1)

    @pl.loop(1, n)
    def _(step):
        dest = lax.rem(me + step, n)
        for group in range(groups):
            first_copy(me, dest, group).wait_send()
        for chunk in range(chunks):
            second_copy(me, dest, chunk).wait_send()

    for chunk in range(chunks):
        collect(chunk)
    for chunk in range(chunks):
        for step in range(1, ENS):
            other = lax.rem(member + step, ENS)
            member_copy(member, other, chunk).wait_send()
            slope_copy(member, other, chunk).wait_send()
        out_copy(0, chunk).wait()
        out_copy(1, chunk).wait()


def copy_kernel(pieces, pred_hbm, grad_hbm, pred_out, grad_out, sem):
    part = pred_hbm.shape[0] // pieces
    copies = []
    for which, (source, dest) in enumerate(((pred_hbm, pred_out), (grad_hbm, grad_out))):
        for i in range(pieces):
            at = pl.ds(i * part, part)
            copies.append(pltpu.make_async_copy(source.at[at], dest.at[at], sem.at[which, i]))
    for copy in copies:
        copy.start()
    for copy in copies:
        copy.wait()


def body(field, target, slot_orders, analysis, synthesis, degree_filter):
    lat, chan, lon = field.shape[1:]
    slots, lat_total, degrees = analysis.shape
    n = lax.axis_size("polar")
    group_count = lax.axis_size("ens") // ENS
    groups = -(-slots // TILE)
    per_group = -(-slots // groups)
    padded = groups * TILE
    per_send = max(d for d in range(1, n + 1) if n % d == 0 and (d == 1 or d * TILE <= 128))
    pair = 2 if lat % 2 == 0 else 1
    chunks = lat // pair
    rows = pair * chan
    quarter = rows // ENS
    forward, inverse = order_tables(lon, degrees)
    observed = target
    filters = degree_filter
    if group_count > 1:
        start = lax.axis_index("ens") // ENS * chan
        observed = lax.dynamic_slice_in_dim(target, start, chan, 1)
        filters = lax.dynamic_slice_in_dim(degree_filter, start, chan, 0)
    sizes = (n, lat, chan, slots, groups, per_group, degrees, per_send, pair)
    vmem = pl.BlockSpec(memory_space=pltpu.VMEM)
    smem = pl.BlockSpec(memory_space=pltpu.SMEM)
    anywhere = pl.BlockSpec(memory_space=pl.ANY)
    dma = pltpu.SemaphoreType.DMA
    flat = jax.ShapeDtypeStruct((lat * chan, lon), BF16)
    prediction, gradient = pl.pallas_call(
        functools.partial(kernel, sizes),
        out_shape=(flat, flat),
        in_specs=[anywhere, smem, vmem, vmem] + [anywhere] * 5,
        out_specs=(anywhere, anywhere),
        scratch_shapes=[
            pltpu.VMEM((lat * chan, lon), BF16),
            pltpu.VMEM(forward.shape, BF16),
            pltpu.VMEM(inverse.shape, BF16),
            pltpu.VMEM((lat * chan, lon), BF16),
            pltpu.VMEM(analysis.shape, BF16),
            pltpu.VMEM((slots, lat_total, degrees), BF16),
            pltpu.VMEM((slots, degrees, lat_total), BF16),
            pltpu.VMEM((degrees, 2 * LANES), F32),
            pltpu.VMEM((2, n * padded, lon), BF16),
            pltpu.VMEM((groups, n, TILE, 2 * lat * chan), BF16),
            pltpu.VMEM((groups, n, TILE, 2 * lat * chan), BF16),
            pltpu.VMEM((lat_total * TILE, LANES), F32),
            pltpu.VMEM((lat_total * TILE, LANES), F32),
            pltpu.VMEM((groups * lat_total * TILE, LANES), F32),
            pltpu.VMEM((groups * lat_total * TILE, LANES), F32),
            pltpu.VMEM((chunks, n, padded, 2 * rows), BF16),
            pltpu.VMEM((chunks, n, padded, 2 * rows), BF16),
            pltpu.VMEM((lat * chan, lon), BF16),
            pltpu.VMEM((chunks, ENS, quarter, lon), BF16),
            pltpu.VMEM((chunks, ENS, quarter, lon), BF16),
            pltpu.VMEM((lat * chan, lon), BF16),
            dma((6,)),
            dma((2, chunks)),
            dma((groups, n)),
            dma((groups, n)),
            dma((chunks, n)),
            dma((chunks, n)),
            dma((chunks, ENS)),
            dma((chunks, ENS)),
            dma((chunks, ENS)),
            dma((chunks, ENS)),
        ],
        compiler_params=pltpu.CompilerParams(
            collective_id=0, has_side_effects=True, vmem_limit_bytes=56 * 1024 * 1024
        ),
    )(
        field.reshape(lat * chan, lon),
        slot_orders,
        slot_orders.reshape(1, -1),
        filters,
        forward,
        inverse,
        observed.reshape(lat * chan, lon),
        analysis,
        jnp.swapaxes(synthesis, 1, 2),
    )
    pieces = lat
    prediction, gradient = pl.pallas_call(
        functools.partial(copy_kernel, pieces),
        out_shape=(flat, flat),
        in_specs=[anywhere] * 2,
        out_specs=(anywhere, anywhere),
        scratch_shapes=[dma((2, pieces))],
    )(prediction, gradient)
    return prediction.reshape(field.shape), gradient.reshape(field.shape)


def solution(mesh):
    in_specs = (
        P("ens", "polar", None, None),
        P("polar", None, None),
        P(),
        P("polar", None, None),
        P("polar", None, None),
        P(),
    )
    out_specs = (P("ens", "polar", None, None), P("ens", "polar", None, None))
    return jax.shard_map(body, mesh=mesh, in_specs=in_specs, out_specs=out_specs, check_vma=False)
```

```python
import functools
import math

import jax
import jax.numpy as jnp
import numpy as np
from jax import lax
from jax.experimental import pallas as pl
from jax.experimental.pallas import tpu as pltpu
from jax.sharding import PartitionSpec as P

ENS = 4
SMOOTH_SQ = 0.25
MESH = pl.DeviceIdType.MESH
F32 = jnp.float32
BF16 = jnp.bfloat16
LANES = 128
TILE = 16


def order_tables(lon_count, degree_total):
    phase = np.arange(degree_total)[:, None] * np.arange(lon_count)[None, :] % lon_count
    angle = phase.astype(np.float32) * np.float32(2.0 * math.pi / lon_count)
    paired = np.stack([np.cos(angle), -np.sin(angle)])
    forward = jnp.asarray((paired / np.float32(math.sqrt(lon_count))).astype(BF16))
    inverse = jnp.asarray((paired / np.float32(math.sqrt(degree_total))).astype(BF16))
    return forward, inverse


def nt_dot(a, b):
    return lax.dot_general(a, b, (((1,), (1,)), ((), ())), preferred_element_type=F32)


def kernel_slope(diff):
    return diff * lax.rsqrt(diff * diff + SMOOTH_SQ)


def kernel(
    sizes,
    field_hbm, orders_ref, order_row_ref, filter_ref, forward_hbm,
    inverse_hbm, target_hbm, analysis_hbm, synthesis_ref_hbm,
    pred_hbm, grad_hbm,
    field_ref, forward_ref, inverse_tab, target_ref, analysis_ref, synthesis_ref,
    analysis_t, filter_t, inverse_rows,
    send1, recv1, x0, x1, b0, b1, send2, recv2, pred_ref, members, slopes, grad_in,
    local_sem, out_sem, send1_sem, recv1_sem, send2_sem, recv2_sem,
    send3_sem, recv3_sem, send4_sem, recv4_sem,
):
    n, lat, chan, slots, groups, per_group, degrees, per_send, pair = sizes
    lat_total = n * lat
    padded = groups * TILE
    me = lax.axis_index("polar")
    slab = lax.axis_index("ens")
    member = lax.rem(slab, ENS)
    group_base = slab - member
    chunks = lat // pair
    rows = pair * chan
    quarter = rows // ENS

    pairs_in = [
        (forward_hbm, forward_ref),
        (field_hbm, field_ref),
        (analysis_hbm, analysis_ref),
        (inverse_hbm, inverse_tab),
        (synthesis_ref_hbm, synthesis_ref),
        (target_hbm, target_ref),
    ]
    local = [
        pltpu.make_async_copy(src, dst, local_sem.at[i]) for i, (src, dst) in enumerate(pairs_in)
    ]
    for copy in local:
        copy.start()

    barrier = pltpu.get_barrier_semaphore()

    @pl.loop(1, n)
    def _(step):
        pl.semaphore_signal(
            barrier, inc=1, device_id={"polar": lax.rem(me + step, n)}, device_id_type=MESH
        )

    for step in range(1, ENS):
        other = group_base + lax.rem(member + step, ENS)
        pl.semaphore_signal(barrier, inc=1, device_id={"ens": other}, device_id_type=MESH)

    def first_copy(slot, dest, group):
        return pltpu.make_async_remote_copy(
            src_ref=send1.at[group, dest],
            dst_ref=recv1.at[group, slot],
            send_sem=send1_sem.at[group, dest],
            recv_sem=recv1_sem.at[group, slot],
            device_id={"polar": dest},
            device_id_type=MESH,
        )

    def second_copy(slot, dest, chunk, part):
        sem = part if chunk == 0 else groups + chunk - 1
        at = pl.ds(part * TILE, TILE) if chunk == 0 else pl.ds(0, padded)
        return pltpu.make_async_remote_copy(
            src_ref=send2.at[chunk, dest, at],
            dst_ref=recv2.at[chunk, slot, at],
            send_sem=send2_sem.at[sem, dest],
            recv_sem=recv2_sem.at[sem, slot],
            device_id={"polar": dest},
            device_id_type=MESH,
        )

    def parts_of(chunk):
        return range(groups if chunk == 0 else 1)

    def row_start(chunk, owner):
        return pl.multiple_of(chunk * rows + owner * quarter, TILE)

    def member_copy(slot, dest, chunk):
        return pltpu.make_async_remote_copy(
            src_ref=pred_ref.at[pl.ds(row_start(chunk, dest), quarter)],
            dst_ref=members.at[chunk, slot],
            send_sem=send3_sem.at[chunk, dest],
            recv_sem=recv3_sem.at[chunk, slot],
            device_id={"ens": group_base + dest},
            device_id_type=MESH,
        )

    def slope_copy(slot, dest, chunk):
        return pltpu.make_async_remote_copy(
            src_ref=slopes.at[chunk, dest],
            dst_ref=grad_in.at[pl.ds(row_start(chunk, slot), quarter)],
            send_sem=send4_sem.at[chunk, dest],
            recv_sem=recv4_sem.at[chunk, slot],
            device_id={"ens": group_base + dest},
            device_id_type=MESH,
        )

    def out_copy(which, chunk):
        source, dest = ((pred_ref, pred_hbm), (grad_in, grad_hbm))[which]
        at = pl.ds(chunk * rows, rows)
        return pltpu.make_async_copy(source.at[at], dest.at[at], out_sem.at[which, chunk])

    order_row = order_row_ref[...].astype(F32)

    def one_hot(device, group, rank):
        slot = group * per_group + rank
        live = (rank < per_group) & (slot < slots)
        slot = jnp.where(live, device * slots + slot, -1)
        ids = lax.broadcasted_iota(jnp.int32, (slot.shape[0], order_row.shape[1]), 1)
        picked = jnp.where(ids == slot, order_row + 1.0, 0.0)
        order = jnp.sum(picked, axis=1, keepdims=True) - 1.0
        ids = lax.broadcasted_iota(jnp.int32, (slot.shape[0], degrees), 1).astype(F32)
        return jnp.where(ids == order, 1.0, 0.0).astype(BF16)

    def selected(hot, table):
        return jnp.dot(hot, table, preferred_element_type=F32).astype(BF16)

    batches = n // per_send
    span = per_send * TILE

    def column(count):
        return lax.broadcasted_iota(jnp.int32, (count, 1), 0)

    def spectral(group, batch):
        first = batch * per_send
        position = column(span)
        hot = one_hot(first + position // TILE, group, lax.rem(position, TILE))
        table = jnp.concatenate([selected(hot, forward_ref[0]), selected(hot, forward_ref[1])], 0)
        values = nt_dot(table, field_ref[...])
        both = jnp.concatenate([values[:span], values[span:]], axis=1).astype(BF16)
        for j in range(per_send):
            send1[group, first + j] = both[j * TILE : (j + 1) * TILE]

    def dispatch(group, batch):
        first = batch * per_send

        @pl.loop(0, per_send)
        def _(j):
            dest = first + lax.rem(me + 1 + j, per_send)

            @pl.when(dest != me)
            def _():
                first_copy(me, dest, group).start()

    local[0].wait()
    local[1].wait()
    spectral(0, 0)
    pl.semaphore_wait(barrier, n - 1 + ENS - 1)
    dispatch(0, 0)

    @pl.loop(1, groups * batches)
    def _(i):
        spectral(i // batches, lax.rem(i, batches))
        dispatch(i // batches, lax.rem(i, batches))

    def turn_analysis(group):
        @pl.loop(group * per_group, min(slots, (group + 1) * per_group))
        def _(s):
            order = orders_ref[me * slots + s]
            table = jnp.transpose(analysis_ref[s].astype(F32))
            degree = lax.broadcasted_iota(jnp.int32, table.shape, 0)
            analysis_t[s] = jnp.where(degree >= order, table, 0.0).astype(BF16)

    turned = jnp.transpose(filter_ref[...])
    filter_t[...] = jnp.zeros_like(filter_t)
    filter_t[:, 0:chan] = turned
    filter_t[:, LANES : LANES + chan] = turned
    b0[...] = jnp.zeros_like(b0)
    b1[...] = jnp.zeros_like(b1)
    local[2].wait()
    local[4].wait()

    def turn_inverse():
        span = per_send * padded

        @pl.loop(0, batches)
        def _(batch):
            position = column(span)
            place = lax.rem(position, padded)
            hot = one_hot(batch * per_send + position // padded, place // TILE, lax.rem(place, TILE))
            at = pl.ds(pl.multiple_of(batch * span, TILE), span)
            inverse_rows[0, at] = selected(hot, inverse_tab[0])
            inverse_rows[1, at] = selected(hot, inverse_tab[1])

    for group in range(groups):
        turn_analysis(group)
        recv1[group, me] = send1[group, me]

        @pl.loop(0, n)
        def _(src):
            @pl.when(src != me)
            def _():
                first_copy(src, src, group).wait_recv()

            block = recv1[group, src].astype(F32)
            for t in range(lat):
                at = pl.ds(pl.multiple_of((src * lat + t) * TILE, TILE), TILE)
                x0[at, 0:chan] = block[:, t * chan : (t + 1) * chan]
                x1[at, 0:chan] = block[:, (lat + t) * chan : (lat + t + 1) * chan]

        base = group * lat_total * TILE

        def legendre(rank, carry):
            s = group * per_group + rank
            at = pl.ds(rank, lat_total, stride=TILE)
            values = jnp.concatenate([x0[at, :], x1[at, :]], axis=1).astype(BF16)
            coeffs = jnp.dot(analysis_t[s], values, preferred_element_type=F32)
            scaled = (coeffs * filter_t[...]).astype(BF16)
            bands = jnp.dot(synthesis_ref[s], scaled, preferred_element_type=F32)
            out = pl.ds(base + rank, lat_total, stride=TILE)
            b0[out, :] = bands[:, :LANES]
            b1[out, :] = bands[:, LANES:]
            return carry

        count = min(per_group, slots - group * per_group)
        unroll = max(u for u in (1, 2, 3, 4, 5) if count % u == 0)
        lax.fori_loop(0, count, legendre, 0, unroll=unroll)

        for chunk in range(chunks):

            @pl.loop(0, n)
            def _(step):
                dest = lax.rem(me + 1 + step, n)
                parts = []
                for source in (b0, b1):
                    for t in range(pair):
                        at = base + (dest * lat + chunk * pair + t) * TILE
                        parts.append(source[pl.ds(pl.multiple_of(at, TILE), TILE), 0:chan])
                send2[chunk, dest, group * TILE : (group + 1) * TILE, :] = jnp.concatenate(
                    parts, axis=1
                ).astype(BF16)

                if chunk == 0 or group == groups - 1:

                    @pl.when(dest != me)
                    def _():
                        second_copy(me, dest, chunk, group).start()

        if group == 0:
            local[3].wait()
            local[5].wait()
            turn_inverse()

    def invert(chunk):
        recv2[chunk, me] = send2[chunk, me]

        @pl.loop(1, n)
        def _(step):
            src = lax.rem(me + step, n)
            for part in parts_of(chunk):
                second_copy(src, src, chunk, part).wait_recv()

        bands = recv2[chunk].reshape(n * padded, 2 * rows)
        turned = jnp.transpose(bands.astype(F32)).astype(BF16)
        synth = jnp.dot(turned[:rows], inverse_rows[0], preferred_element_type=F32)
        synth = synth + jnp.dot(turned[rows:], inverse_rows[1], preferred_element_type=F32)
        at = pl.ds(chunk * rows, rows)
        pred_ref[at, :] = (field_ref[at, :].astype(F32) + synth).astype(BF16)
        for step in range(1, ENS):
            member_copy(member, lax.rem(member + step, ENS), chunk).start()
        out_copy(0, chunk).start()

    def score(chunk):
        own = pl.ds(row_start(chunk, member), quarter)
        members[chunk, member] = pred_ref[own, :]
        for step in range(1, ENS):
            source = lax.rem(member + step, ENS)
            member_copy(source, source, chunk).wait_recv()

        @pl.loop(0, quarter // TILE)
        def _(i):
            start = pl.multiple_of(i * TILE, TILE)
            at = pl.ds(start, TILE)
            seen = target_ref[pl.ds(row_start(chunk, member) + start, TILE), :].astype(F32)
            values = [members[chunk, e, at, :].astype(F32) for e in range(ENS)]
            pairs = [jnp.zeros_like(seen) for _ in range(ENS)]
            for a in range(ENS):
                for b in range(a + 1, ENS):
                    slope = kernel_slope(values[a] - values[b])
                    pairs[a] = pairs[a] + slope
                    pairs[b] = pairs[b] - slope
            for e in range(ENS):
                total = kernel_slope(values[e] - seen) - pairs[e] / ENS
                slopes[chunk, e, at, :] = total.astype(BF16)

        for step in range(1, ENS):
            slope_copy(member, lax.rem(member + step, ENS), chunk).start()
        grad_in[own, :] = slopes[chunk, member]

    def collect(chunk):
        for step in range(1, ENS):
            other = lax.rem(member + step, ENS)
            slope_copy(other, other, chunk).wait_recv()
        out_copy(1, chunk).start()

    for chunk in range(chunks):
        invert(chunk)
        if chunk:
            score(chunk - 1)
    score(chunks - 1)

    @pl.loop(1, n)
    def _(step):
        dest = lax.rem(me + step, n)
        for group in range(groups):
            first_copy(me, dest, group).wait_send()
        for chunk in range(chunks):
            for part in parts_of(chunk):
                second_copy(me, dest, chunk, part).wait_send()

    for chunk in range(chunks):
        collect(chunk)
    for chunk in range(chunks):
        for step in range(1, ENS):
            other = lax.rem(member + step, ENS)
            member_copy(member, other, chunk).wait_send()
            slope_copy(member, other, chunk).wait_send()
        out_copy(0, chunk).wait()
        out_copy(1, chunk).wait()


def body(field, target, slot_orders, analysis, synthesis, degree_filter):
    lat, chan, lon = field.shape[1:]
    slots, lat_total, degrees = analysis.shape
    n = lax.axis_size("polar")
    group_count = lax.axis_size("ens") // ENS
    groups = -(-slots // TILE)
    per_group = -(-slots // groups)
    padded = groups * TILE
    per_send = max(d for d in range(1, n + 1) if n % d == 0 and (d == 1 or d * TILE <= 128))
    pair = 2 if lat % 2 == 0 else 1
    chunks = lat // pair
    rows = pair * chan
    quarter = rows // ENS
    forward, inverse = order_tables(lon, degrees)
    observed = target
    filters = degree_filter
    if group_count > 1:
        start = lax.axis_index("ens") // ENS * chan
        observed = lax.dynamic_slice_in_dim(target, start, chan, 1)
        filters = lax.dynamic_slice_in_dim(degree_filter, start, chan, 0)
    sizes = (n, lat, chan, slots, groups, per_group, degrees, per_send, pair)
    vmem = pl.BlockSpec(memory_space=pltpu.VMEM)
    smem = pl.BlockSpec(memory_space=pltpu.SMEM)
    anywhere = pl.BlockSpec(memory_space=pl.ANY)
    dma = pltpu.SemaphoreType.DMA
    flat = jax.ShapeDtypeStruct((lat * chan, lon), BF16)
    prediction, gradient = pl.pallas_call(
        functools.partial(kernel, sizes),
        out_shape=(flat, flat),
        in_specs=[anywhere, smem, vmem, vmem] + [anywhere] * 5,
        out_specs=(anywhere, anywhere),
        scratch_shapes=[
            pltpu.VMEM((lat * chan, lon), BF16),
            pltpu.VMEM(forward.shape, BF16),
            pltpu.VMEM(inverse.shape, BF16),
            pltpu.VMEM((lat * chan, lon), BF16),
            pltpu.VMEM(analysis.shape, BF16),
            pltpu.VMEM((slots, lat_total, degrees), BF16),
            pltpu.VMEM((slots, degrees, lat_total), BF16),
            pltpu.VMEM((degrees, 2 * LANES), F32),
            pltpu.VMEM((2, n * padded, lon), BF16),
            pltpu.VMEM((groups, n, TILE, 2 * lat * chan), BF16),
            pltpu.VMEM((groups, n, TILE, 2 * lat * chan), BF16),
            pltpu.VMEM((lat_total * TILE, LANES), F32),
            pltpu.VMEM((lat_total * TILE, LANES), F32),
            pltpu.VMEM((groups * lat_total * TILE, LANES), F32),
            pltpu.VMEM((groups * lat_total * TILE, LANES), F32),
            pltpu.VMEM((chunks, n, padded, 2 * rows), BF16),
            pltpu.VMEM((chunks, n, padded, 2 * rows), BF16),
            pltpu.VMEM((lat * chan, lon), BF16),
            pltpu.VMEM((chunks, ENS, quarter, lon), BF16),
            pltpu.VMEM((chunks, ENS, quarter, lon), BF16),
            pltpu.VMEM((lat * chan, lon), BF16),
            dma((6,)),
            dma((2, chunks)),
            dma((groups, n)),
            dma((groups, n)),
            dma((groups + chunks - 1, n)),
            dma((groups + chunks - 1, n)),
            dma((chunks, ENS)),
            dma((chunks, ENS)),
            dma((chunks, ENS)),
            dma((chunks, ENS)),
        ],
        compiler_params=pltpu.CompilerParams(
            collective_id=0, has_side_effects=True, vmem_limit_bytes=56 * 1024 * 1024
        ),
    )(
        field.reshape(lat * chan, lon),
        slot_orders,
        slot_orders.reshape(1, -1),
        filters,
        forward,
        inverse,
        observed.reshape(lat * chan, lon),
        analysis,
        jnp.swapaxes(synthesis, 1, 2),
    )
    return prediction.reshape(field.shape), gradient.reshape(field.shape)


def solution(mesh):
    in_specs = (
        P("ens", "polar", None, None),
        P("polar", None, None),
        P(),
        P("polar", None, None),
        P("polar", None, None),
        P(),
    )
    out_specs = (P("ens", "polar", None, None), P("ens", "polar", None, None))
    return jax.shard_map(body, mesh=mesh, in_specs=in_specs, out_specs=out_specs, check_vma=False)
```

```python
import functools
import math

import jax
import jax.numpy as jnp
import numpy as np
from jax import lax
from jax.experimental import pallas as pl
from jax.experimental.pallas import tpu as pltpu
from jax.sharding import PartitionSpec as P

ENS = 4
SMOOTH_SQ = 0.25
MESH = pl.DeviceIdType.MESH
F32 = jnp.float32
BF16 = jnp.bfloat16
LANES = 128
TILE = 16


def order_tables(lon_count, degree_total):
    phase = np.arange(degree_total)[:, None] * np.arange(lon_count)[None, :] % lon_count
    angle = phase.astype(np.float32) * np.float32(2.0 * math.pi / lon_count)
    paired = np.stack([np.cos(angle), -np.sin(angle)])
    forward = jnp.asarray((paired / np.float32(math.sqrt(lon_count))).astype(BF16))
    inverse = jnp.asarray((paired / np.float32(math.sqrt(degree_total))).astype(BF16))
    return forward, inverse


def nt_dot(a, b):
    return lax.dot_general(a, b, (((1,), (1,)), ((), ())), preferred_element_type=F32)


def kernel_slope(diff):
    return diff * lax.rsqrt(diff * diff + SMOOTH_SQ)


def kernel(
    sizes,
    field_hbm, orders_ref, order_row_ref, filter_ref, forward_hbm,
    inverse_hbm, target_hbm, analysis_hbm, synthesis_ref_hbm,
    pred_hbm, grad_hbm,
    field_ref, forward_ref, inverse_tab, target_ref, analysis_ref, synthesis_ref,
    analysis_t, filter_t, inverse_rows,
    send1, recv1, x0, x1, b0, b1, send2, recv2, pred_ref, members, slopes, grad_in,
    local_sem, out_sem, send1_sem, recv1_sem, send2_sem, recv2_sem,
    send3_sem, recv3_sem, send4_sem, recv4_sem,
):
    n, lat, chan, slots, groups, per_group, degrees, per_send, pair = sizes
    lat_total = n * lat
    padded = groups * TILE
    me = lax.axis_index("polar")
    slab = lax.axis_index("ens")
    member = lax.rem(slab, ENS)
    group_base = slab - member
    chunks = lat // pair
    rows = pair * chan
    quarter = rows // ENS

    pairs_in = [
        (forward_hbm, forward_ref),
        (field_hbm, field_ref),
        (analysis_hbm, analysis_ref),
        (inverse_hbm, inverse_tab),
        (synthesis_ref_hbm, synthesis_ref),
        (target_hbm, target_ref),
    ]
    local = [
        pltpu.make_async_copy(src, dst, local_sem.at[i]) for i, (src, dst) in enumerate(pairs_in)
    ]
    for copy in local:
        copy.start()

    barrier = pltpu.get_barrier_semaphore()

    @pl.loop(1, n)
    def _(step):
        pl.semaphore_signal(
            barrier, inc=1, device_id={"polar": lax.rem(me + step, n)}, device_id_type=MESH
        )

    for step in range(1, ENS):
        other = group_base + lax.rem(member + step, ENS)
        pl.semaphore_signal(barrier, inc=1, device_id={"ens": other}, device_id_type=MESH)

    def first_copy(slot, dest, group):
        return pltpu.make_async_remote_copy(
            src_ref=send1.at[group, dest],
            dst_ref=recv1.at[group, slot],
            send_sem=send1_sem.at[group, dest],
            recv_sem=recv1_sem.at[group, slot],
            device_id={"polar": dest},
            device_id_type=MESH,
        )

    def second_copy(slot, dest, chunk, part):
        sem = part if chunk == 0 else groups + chunk - 1
        at = pl.ds(part * TILE, TILE) if chunk == 0 else pl.ds(0, padded)
        return pltpu.make_async_remote_copy(
            src_ref=send2.at[chunk, dest, at],
            dst_ref=recv2.at[chunk, slot, at],
            send_sem=send2_sem.at[sem, dest],
            recv_sem=recv2_sem.at[sem, slot],
            device_id={"polar": dest},
            device_id_type=MESH,
        )

    def parts_of(chunk):
        return range(groups if chunk == 0 else 1)

    def row_start(chunk, owner):
        return pl.multiple_of(chunk * rows + owner * quarter, TILE)

    def member_copy(slot, dest, chunk):
        return pltpu.make_async_remote_copy(
            src_ref=pred_ref.at[pl.ds(row_start(chunk, dest), quarter)],
            dst_ref=members.at[chunk, slot],
            send_sem=send3_sem.at[chunk, dest],
            recv_sem=recv3_sem.at[chunk, slot],
            device_id={"ens": group_base + dest},
            device_id_type=MESH,
        )

    def slope_copy(slot, dest, chunk):
        return pltpu.make_async_remote_copy(
            src_ref=slopes.at[chunk, dest],
            dst_ref=grad_in.at[pl.ds(row_start(chunk, slot), quarter)],
            send_sem=send4_sem.at[chunk, dest],
            recv_sem=recv4_sem.at[chunk, slot],
            device_id={"ens": group_base + dest},
            device_id_type=MESH,
        )

    def out_copy(which, chunk):
        source, dest = ((pred_ref, pred_hbm), (grad_in, grad_hbm))[which]
        at = pl.ds(chunk * rows, rows)
        return pltpu.make_async_copy(source.at[at], dest.at[at], out_sem.at[which, chunk])

    order_row = order_row_ref[...].astype(F32)

    def one_hot(device, group, rank):
        slot = group * per_group + rank
        live = (rank < per_group) & (slot < slots)
        slot = jnp.where(live, device * slots + slot, -1)
        ids = lax.broadcasted_iota(jnp.int32, (slot.shape[0], order_row.shape[1]), 1)
        picked = jnp.where(ids == slot, order_row + 1.0, 0.0)
        order = jnp.sum(picked, axis=1, keepdims=True) - 1.0
        ids = lax.broadcasted_iota(jnp.int32, (slot.shape[0], degrees), 1).astype(F32)
        return jnp.where(ids == order, 1.0, 0.0).astype(BF16)

    def selected(hot, table):
        return jnp.dot(hot, table, preferred_element_type=F32).astype(BF16)

    batches = n // per_send
    span = per_send * TILE

    def column(count):
        return lax.broadcasted_iota(jnp.int32, (count, 1), 0)

    def spectral(group, batch):
        first = batch * per_send
        position = column(span)
        hot = one_hot(first + position // TILE, group, lax.rem(position, TILE))
        table = jnp.concatenate([selected(hot, forward_ref[0]), selected(hot, forward_ref[1])], 0)
        values = nt_dot(table, field_ref[...])
        both = jnp.concatenate([values[:span], values[span:]], axis=1).astype(BF16)
        for j in range(per_send):
            send1[group, first + j] = both[j * TILE : (j + 1) * TILE]

    def dispatch(group, batch):
        first = batch * per_send

        @pl.loop(0, per_send)
        def _(j):
            dest = first + lax.rem(me + 1 + j, per_send)

            @pl.when(dest != me)
            def _():
                first_copy(me, dest, group).start()

    local[0].wait()
    local[1].wait()
    spectral(0, 0)
    pl.semaphore_wait(barrier, n - 1 + ENS - 1)
    dispatch(0, 0)

    @pl.loop(1, groups * batches)
    def _(i):
        spectral(i // batches, lax.rem(i, batches))
        dispatch(i // batches, lax.rem(i, batches))

    def turn_analysis(group):
        @pl.loop(group * per_group, min(slots, (group + 1) * per_group))
        def _(s):
            order = orders_ref[me * slots + s]
            table = jnp.transpose(analysis_ref[s].astype(F32))
            degree = lax.broadcasted_iota(jnp.int32, table.shape, 0)
            analysis_t[s] = jnp.where(degree >= order, table, 0.0).astype(BF16)

    turned = jnp.transpose(filter_ref[...])
    filter_t[...] = jnp.zeros_like(filter_t)
    filter_t[:, 0:chan] = turned
    filter_t[:, LANES : LANES + chan] = turned
    b0[...] = jnp.zeros_like(b0)
    b1[...] = jnp.zeros_like(b1)
    local[2].wait()
    local[4].wait()

    def turn_inverse():
        span = per_send * padded

        @pl.loop(0, batches)
        def _(batch):
            position = column(span)
            place = lax.rem(position, padded)
            hot = one_hot(batch * per_send + position // padded, place // TILE, lax.rem(place, TILE))
            at = pl.ds(pl.multiple_of(batch * span, TILE), span)
            inverse_rows[0, at] = selected(hot, inverse_tab[0])
            inverse_rows[1, at] = selected(hot, inverse_tab[1])

    for group in range(groups):
        turn_analysis(group)
        recv1[group, me] = send1[group, me]

        @pl.loop(0, n)
        def _(src):
            @pl.when(src != me)
            def _():
                first_copy(src, src, group).wait_recv()

            block = recv1[group, src].astype(F32)
            for t in range(lat):
                at = pl.ds(pl.multiple_of((src * lat + t) * TILE, TILE), TILE)
                x0[at, 0:chan] = block[:, t * chan : (t + 1) * chan]
                x1[at, 0:chan] = block[:, (lat + t) * chan : (lat + t + 1) * chan]

        base = group * lat_total * TILE

        def legendre(rank, carry):
            s = group * per_group + rank
            at = pl.ds(rank, lat_total, stride=TILE)
            values = jnp.concatenate([x0[at, :], x1[at, :]], axis=1).astype(BF16)
            coeffs = jnp.dot(analysis_t[s], values, preferred_element_type=F32)
            scaled = (coeffs * filter_t[...]).astype(BF16)
            bands = jnp.dot(synthesis_ref[s], scaled, preferred_element_type=F32)
            out = pl.ds(base + rank, lat_total, stride=TILE)
            b0[out, :] = bands[:, :LANES]
            b1[out, :] = bands[:, LANES:]
            return carry

        count = min(per_group, slots - group * per_group)
        unroll = max(u for u in (1, 2, 3, 4, 5) if count % u == 0)
        lax.fori_loop(0, count, legendre, 0, unroll=unroll)

        for chunk in range(chunks):

            @pl.loop(0, n)
            def _(step):
                dest = lax.rem(me + 1 + step, n)
                parts = []
                for source in (b0, b1):
                    for t in range(pair):
                        at = base + (dest * lat + chunk * pair + t) * TILE
                        parts.append(source[pl.ds(pl.multiple_of(at, TILE), TILE), 0:chan])
                send2[chunk, dest, group * TILE : (group + 1) * TILE, :] = jnp.concatenate(
                    parts, axis=1
                ).astype(BF16)

                if chunk == 0 or group == groups - 1:

                    @pl.when(dest != me)
                    def _():
                        second_copy(me, dest, chunk, group).start()

        if group == 0:
            local[3].wait()
            local[5].wait()
            turn_inverse()

    def invert(chunk):
        recv2[chunk, me] = send2[chunk, me]

        @pl.loop(1, n)
        def _(step):
            src = lax.rem(me + step, n)
            for part in parts_of(chunk):
                second_copy(src, src, chunk, part).wait_recv()

        bands = recv2[chunk].reshape(n * padded, 2 * rows)
        turned = jnp.transpose(bands.astype(F32)).astype(BF16)
        synth = jnp.dot(turned[:rows], inverse_rows[0], preferred_element_type=F32)
        synth = synth + jnp.dot(turned[rows:], inverse_rows[1], preferred_element_type=F32)
        at = pl.ds(chunk * rows, rows)
        pred_ref[at, :] = (field_ref[at, :].astype(F32) + synth).astype(BF16)
        for step in range(1, ENS):
            member_copy(member, lax.rem(member + step, ENS), chunk).start()
        out_copy(0, chunk).start()

    def score(chunk):
        own = pl.ds(row_start(chunk, member), quarter)
        members[chunk, member] = pred_ref[own, :]
        for step in range(1, ENS):
            source = lax.rem(member + step, ENS)
            member_copy(source, source, chunk).wait_recv()

        @pl.loop(0, quarter // TILE)
        def _(i):
            start = pl.multiple_of(i * TILE, TILE)
            at = pl.ds(start, TILE)
            seen = target_ref[pl.ds(row_start(chunk, member) + start, TILE), :].astype(F32)
            values = [members[chunk, e, at, :].astype(F32) for e in range(ENS)]
            pairs = [jnp.zeros_like(seen) for _ in range(ENS)]
            for a in range(ENS):
                for b in range(a + 1, ENS):
                    slope = kernel_slope(values[a] - values[b])
                    pairs[a] = pairs[a] + slope
                    pairs[b] = pairs[b] - slope
            for e in range(ENS):
                total = kernel_slope(values[e] - seen) - pairs[e] / ENS
                slopes[chunk, e, at, :] = total.astype(BF16)

        for step in range(1, ENS):
            slope_copy(member, lax.rem(member + step, ENS), chunk).start()
        grad_in[own, :] = slopes[chunk, member]

    def collect(chunk):
        for step in range(1, ENS):
            other = lax.rem(member + step, ENS)
            slope_copy(other, other, chunk).wait_recv()
        out_copy(1, chunk).start()

    for chunk in range(chunks):
        invert(chunk)
        score(chunk)

    @pl.loop(1, n)
    def _(step):
        dest = lax.rem(me + step, n)
        for group in range(groups):
            first_copy(me, dest, group).wait_send()
        for chunk in range(chunks):
            for part in parts_of(chunk):
                second_copy(me, dest, chunk, part).wait_send()

    for chunk in range(chunks):
        collect(chunk)
    for chunk in range(chunks):
        for step in range(1, ENS):
            other = lax.rem(member + step, ENS)
            member_copy(member, other, chunk).wait_send()
            slope_copy(member, other, chunk).wait_send()
        out_copy(0, chunk).wait()
        out_copy(1, chunk).wait()


def body(field, target, slot_orders, analysis, synthesis, degree_filter):
    lat, chan, lon = field.shape[1:]
    slots, lat_total, degrees = analysis.shape
    n = lax.axis_size("polar")
    group_count = lax.axis_size("ens") // ENS
    groups = -(-slots // TILE)
    per_group = -(-slots // groups)
    padded = groups * TILE
    per_send = max(d for d in range(1, n + 1) if n % d == 0 and (d == 1 or d * TILE <= 128))
    pair = 2 if lat % 2 == 0 else 1
    chunks = lat // pair
    rows = pair * chan
    quarter = rows // ENS
    forward, inverse = order_tables(lon, degrees)
    observed = target
    filters = degree_filter
    if group_count > 1:
        start = lax.axis_index("ens") // ENS * chan
        observed = lax.dynamic_slice_in_dim(target, start, chan, 1)
        filters = lax.dynamic_slice_in_dim(degree_filter, start, chan, 0)
    sizes = (n, lat, chan, slots, groups, per_group, degrees, per_send, pair)
    vmem = pl.BlockSpec(memory_space=pltpu.VMEM)
    smem = pl.BlockSpec(memory_space=pltpu.SMEM)
    anywhere = pl.BlockSpec(memory_space=pl.ANY)
    dma = pltpu.SemaphoreType.DMA
    flat = jax.ShapeDtypeStruct((lat * chan, lon), BF16)
    prediction, gradient = pl.pallas_call(
        functools.partial(kernel, sizes),
        out_shape=(flat, flat),
        in_specs=[anywhere, smem, vmem, vmem] + [anywhere] * 5,
        out_specs=(anywhere, anywhere),
        scratch_shapes=[
            pltpu.VMEM((lat * chan, lon), BF16),
            pltpu.VMEM(forward.shape, BF16),
            pltpu.VMEM(inverse.shape, BF16),
            pltpu.VMEM((lat * chan, lon), BF16),
            pltpu.VMEM(analysis.shape, BF16),
            pltpu.VMEM((slots, lat_total, degrees), BF16),
            pltpu.VMEM((slots, degrees, lat_total), BF16),
            pltpu.VMEM((degrees, 2 * LANES), F32),
            pltpu.VMEM((2, n * padded, lon), BF16),
            pltpu.VMEM((groups, n, TILE, 2 * lat * chan), BF16),
            pltpu.VMEM((groups, n, TILE, 2 * lat * chan), BF16),
            pltpu.VMEM((lat_total * TILE, LANES), F32),
            pltpu.VMEM((lat_total * TILE, LANES), F32),
            pltpu.VMEM((groups * lat_total * TILE, LANES), F32),
            pltpu.VMEM((groups * lat_total * TILE, LANES), F32),
            pltpu.VMEM((chunks, n, padded, 2 * rows), BF16),
            pltpu.VMEM((chunks, n, padded, 2 * rows), BF16),
            pltpu.VMEM((lat * chan, lon), BF16),
            pltpu.VMEM((chunks, ENS, quarter, lon), BF16),
            pltpu.VMEM((chunks, ENS, quarter, lon), BF16),
            pltpu.VMEM((lat * chan, lon), BF16),
            dma((6,)),
            dma((2, chunks)),
            dma((groups, n)),
            dma((groups, n)),
            dma((groups + chunks - 1, n)),
            dma((groups + chunks - 1, n)),
            dma((chunks, ENS)),
            dma((chunks, ENS)),
            dma((chunks, ENS)),
            dma((chunks, ENS)),
        ],
        compiler_params=pltpu.CompilerParams(
            collective_id=0, has_side_effects=True, vmem_limit_bytes=56 * 1024 * 1024
        ),
    )(
        field.reshape(lat * chan, lon),
        slot_orders,
        slot_orders.reshape(1, -1),
        filters,
        forward,
        inverse,
        observed.reshape(lat * chan, lon),
        analysis,
        jnp.swapaxes(synthesis, 1, 2),
    )
    return prediction.reshape(field.shape), gradient.reshape(field.shape)


def solution(mesh):
    in_specs = (
        P("ens", "polar", None, None),
        P("polar", None, None),
        P(),
        P("polar", None, None),
        P("polar", None, None),
        P(),
    )
    out_specs = (P("ens", "polar", None, None), P("ens", "polar", None, None))
    return jax.shard_map(body, mesh=mesh, in_specs=in_specs, out_specs=out_specs, check_vma=False)
```
